32 devices in a mesh: groups: 2 (over y), dp: 4 (over x, core), tensor: 4 (over z).
Axes of the slice: x: 2, y: 2, z: 4, core: 2. Of those that a mesh axis runs over, the one named last changes fastest.
Arguments:
- attended: bfloat16 [512, 8192], P(('groups', 'dp'), 'tensor'), parts along dimension 0, may hold values from -6 to 6
- output_weight: bfloat16 [8192, 8192], P('tensor'), may hold values from -0.09375 to 0.09375
- down_factor_table: bfloat16 [32, 8192, 64], P('dp', 'tensor'), may hold values from -0.0625 to 0.0625
- up_factor_table: bfloat16 [32, 64, 8192], P('dp', None, 'tensor'), may hold values from -0.75 to 0.75
- request_adapter_index: int32 [512], P(('groups', 'dp')), parts along dimension 0, may hold values from 0 to 31, as said below
- adapter_row_table: int32 [64], P('groups'), parts along dimension 0, may hold values from 0 to 31, as said below
Outputs:
- projected: bfloat16 [512, 8192], P(('groups', 'dp'), 'tensor'), parts along dimension 0
The draws below stay inside these ranges and needn't reach their ends.
There are 2 independent parts, one for each index of `groups`. The reference program is written for one: setup_inputs(seed, part) draws one part's arguments, and reference() takes and returns one part's arrays. A program takes and returns all parts, laid end to end along the dimension named above; an argument that names none is the same for every part. Nothing has to cross between parts.
Inputs may be any that keep to these rules, and one draw needn't show every extreme that they name: adapter_row_table is a permutation of the table rows. `request_adapter_index`: among the 64 requests of one index of dp, at most 32 have row_of in any one group of 8 consecutive table rows starting at a multiple of 8.
All inputs are finite; a program needn't handle non-finite values.
Results may differ from the reference program's by a relative error of at most 0.0075.
Values may be sent and summed in bfloat16 or wider, within the bound.
A program may use at most 128 MiB of HBM per device.

```python
import jax
import jax.numpy as jnp
from jax import lax

MODEL_WIDTH = 8192
ADAPTER_RANK = 64
R_DEV = 64
AD_DEV = 8
ADAPTER_TOTAL = 32
ROWS = 256
CAP = 32
N_DP = 4


def shared_table(key):
    return jax.random.permutation(jax.random.fold_in(key, 11), ADAPTER_TOTAL).astype(jnp.int32)


def draw_adapter_row_table(key, part):
    return shared_table(key)


def draw_request_adapter_index(key, part):
    table = shared_table(key)
    key = jax.random.fold_in(key, 5)
    hot = jax.random.randint(jax.random.fold_in(key, 1), (), 0, N_DP)
    block_keys = jax.random.split(jax.random.fold_in(key, 2), N_DP)

    def one_block(block_key):
        perm = jax.random.permutation(jax.random.fold_in(block_key, 1), N_DP * CAP).astype(jnp.int32)
        owners = perm // CAP
        score = jnp.where(owners == hot, 0, 1) * (N_DP * CAP) + jnp.arange(N_DP * CAP, dtype=jnp.int32)
        order = jnp.argsort(score)
        chosen = owners[order[:R_DEV]]
        shuffle = jax.random.permutation(jax.random.fold_in(block_key, 2), R_DEV)
        chosen = chosen[shuffle]
        local_rows = jax.random.randint(jax.random.fold_in(block_key, 3), (R_DEV,), 0, AD_DEV)
        return chosen * AD_DEV + local_rows
    rows = jax.vmap(one_block)(block_keys).reshape(-1).astype(jnp.int32)
    inverse = jnp.argsort(table).astype(jnp.int32)
    return inverse[rows]


def with_spikes(result, own_key, source, target, blocks, factor):
    def block_of(dim):
        return (jnp.arange(result.shape[dim]) // (result.shape[dim] // blocks)).reshape((-1,) + (1,) * (result.ndim - 1 - dim))

    near = jax.random.permutation(own_key, blocks)[block_of(target)]
    other_side = (block_of(target) + blocks // 2) % blocks
    return jnp.where((block_of(source) == near) | (block_of(source) == other_side), factor * result, result)


def block_scale(own_key, shape, cuts, smallest, top_value):
    loudness = 1.0
    for position, parts in cuts:
        draws = jax.random.uniform(jax.random.fold_in(jax.random.fold_in(own_key, 6), position), (parts,), jnp.float32, smallest / len(cuts), top_value / len(cuts))
        loudness = loudness * jnp.repeat(jnp.exp(draws), shape[position] // parts).reshape((-1,) + (1,) * (len(shape) - 1 - position))
    return loudness


def scatter_about(own_key, extent, spread, limit, cuts=(), kind=jnp.bfloat16):
    values = jax.random.normal(own_key, extent, jnp.float32) * spread
    if len(cuts) > 0:
        values = block_scale(own_key, extent, cuts, -0.22, 0.18) * values
    return jnp.clip(values, min=-limit, max=limit).astype(kind)


def noise_with(rng, extent, spread, most, pieces, heavy, held_as=jnp.bfloat16):
    entries = spread * jax.random.normal(rng, extent, jnp.float32)
    if pieces:
        entries = entries * block_scale(rng, extent, pieces, -0.22, 0.18)
    return jnp.clip(with_spikes(entries, jax.random.fold_in(rng, 3), *heavy), -most, most).astype(held_as)


def setup_inputs(seed: int = 0, part: int = 0) -> dict:
    seeds = jax.random.split(jax.random.key(seed), 7)
    part_splits = jax.random.split(jax.random.fold_in(seeds[6], part), 7)
    return {
        "attended": scatter_about(part_splits[0], (ROWS, MODEL_WIDTH), 1.0, 6.0, ((0, 4), (1, 4))),
        "output_weight": noise_with(seeds[1], (MODEL_WIDTH, MODEL_WIDTH), MODEL_WIDTH ** -0.5, 0.09375, ((0, 4),), (0, 1, 4, 2.0)),
        "down_factor_table": scatter_about(seeds[2], (ADAPTER_TOTAL, MODEL_WIDTH, ADAPTER_RANK), MODEL_WIDTH ** -0.5, 0.0625, ((0, 4), (1, 4))),
        "up_factor_table": scatter_about(seeds[3], (ADAPTER_TOTAL, ADAPTER_RANK, MODEL_WIDTH), ADAPTER_RANK ** -0.5, 0.75, ((0, 4), (2, 4))),
        "request_adapter_index": draw_request_adapter_index(jax.random.fold_in(jax.random.fold_in(seeds[6], part), 71), part),
        "adapter_row_table": draw_adapter_row_table(jax.random.fold_in(jax.random.fold_in(seeds[6], part), 71), part),
    }


def reference(attended, output_weight, down_factor_table, up_factor_table, request_adapter_index, adapter_row_table):
    row_of = adapter_row_table[request_adapter_index].astype(jnp.int32)
    base = jnp.dot(attended, output_weight, preferred_element_type=jnp.float32)

    def low_step(total, table_index):
        adapter_update = jnp.dot(attended, down_factor_table[table_index], preferred_element_type=jnp.float32)
        return total + jnp.where((row_of == table_index)[:, None], adapter_update, 0.0), None

    reduced_state, _ = lax.scan(low_step, jnp.zeros((attended.shape[0], ADAPTER_RANK), jnp.float32), jnp.arange(ADAPTER_TOTAL, dtype=jnp.int32))
    reduced_state = reduced_state.astype(jnp.bfloat16)

    def delta_step(total, table_index):
        adapter_update = jnp.dot(reduced_state, up_factor_table[table_index], preferred_element_type=jnp.float32)
        return total + jnp.where((row_of == table_index)[:, None], adapter_update, 0.0), None

    delta, _ = lax.scan(delta_step, jnp.zeros((attended.shape[0], MODEL_WIDTH), jnp.float32), jnp.arange(ADAPTER_TOTAL, dtype=jnp.int32))
    delta = lax.optimization_barrier(delta.astype(jnp.bfloat16))
    return (base + delta.astype(jnp.float32)).astype(jnp.bfloat16)
```

```python
import functools

import jax
import jax.numpy as jnp
from jax import lax
from jax.experimental import pallas as pl
from jax.experimental.pallas import tpu as pltpu
from jax.sharding import PartitionSpec as P

MESH = pl.DeviceIdType.MESH
F32, BF16 = jnp.float32, jnp.bfloat16


def kernel(
    n_dp, n_t, att_ref, sel_ref, loc_ref, w_ref, down_ref, up_ref, out_ref,
    wbuf, dbuf, ubuf, msg, msg_in, mask, low_own, low_in, dsend, din, ysend, yin, own,
    w_sem, ad_sem, msg_s, msg_r, low_s, low_r, d_s, d_r, y_s, y_r,
):
    d, t = lax.axis_index("dp"), lax.axis_index("tensor")
    depth = att_ref.shape[1]
    nch, chunk = wbuf.shape[1], wbuf.shape[3]
    width = nch * chunk
    cap = msg.shape[1]
    rows_c = n_dp * cap
    half = rows_c // 2
    lanes = low_own.shape[1]
    rank = lanes // 2
    spread_w = dbuf.shape[0]

    def block_at(s):
        down_b = jnp.where(n_t - 1 - s > t, n_t - 1 - s, n_t - 2 - s)
        up_b = jnp.where(s < t, s, s + 1)
        return jnp.where(s == n_t - 1, t, jnp.where(2 * t < n_t - 1, down_b, up_b))

    def w_copy(s, c):
        start = pl.multiple_of(block_at(s) * width + c * chunk, chunk)
        return pltpu.make_async_copy(
            w_ref.at[:, pl.ds(start, chunk)], wbuf.at[s, c], w_sem.at[s, c]
        )

    def fetch(s, _):
        for c in range(nch):
            w_copy(s, c).start()

    down_copy = pltpu.make_async_copy(down_ref, dbuf, ad_sem.at[0])
    up_copy = pltpu.make_async_copy(up_ref, ubuf, ad_sem.at[1])
    fetch(0, None)
    down_copy.start()
    lax.fori_loop(1, max(n_t // 2, 1), fetch, None)
    up_copy.start()
    lax.fori_loop(max(n_t // 2, 1), n_t, fetch, None)

    barrier = pltpu.get_barrier_semaphore()
    for j in range(1, n_dp):
        pl.semaphore_signal(
            barrier, inc=1, device_id={"dp": lax.rem(d + j, n_dp)}, device_id_type=MESH
        )
    for j in range(1, n_t):
        pl.semaphore_signal(
            barrier, inc=1, device_id={"tensor": lax.rem(t + j, n_t)}, device_id_type=MESH
        )
    rows_of = jnp.dot(sel_ref[...], att_ref[...], preferred_element_type=F32)
    msg[:, :, :depth] = rows_of.astype(BF16).reshape(n_dp, cap, depth)
    picks = jnp.dot(sel_ref[...], loc_ref[...], preferred_element_type=F32)
    msg[:, :, depth:] = picks.astype(BF16).reshape(n_dp, cap, lanes)
    msg_in[d] = msg[d]
    pl.semaphore_wait(barrier, n_dp - 1 + n_t - 1)

    def remote(src, dst, send, recv, axis, peer):
        return pltpu.make_async_remote_copy(
            src_ref=src, dst_ref=dst, send_sem=send, recv_sem=recv,
            device_id={axis: peer}, device_id_type=MESH,
        )

    def msg_copy(j):
        peer = lax.rem(d + j, n_dp)
        return remote(msg.at[peer], msg_in.at[d], msg_s.at[j], msg_r.at[d], "dp", peer)

    def msg_arrival(j):
        peer = lax.rem(d + j, n_dp)
        return remote(msg.at[peer], msg_in.at[peer], msg_s.at[j], msg_r.at[peer], "dp", peer)

    def low_copy(j):
        peer = lax.rem(t + j, n_t)
        return remote(low_own, low_in.at[t], low_s.at[j], low_r.at[t], "tensor", peer)

    def low_arrival(j):
        peer = lax.rem(t + j, n_t)
        return remote(low_own, low_in.at[peer], low_s.at[j], low_r.at[peer], "tensor", peer)

    def d_copy(j, c):
        peer = lax.rem(d + j, n_dp)
        return remote(
            dsend.at[peer, c], din.at[d, c], d_s.at[j, c], d_r.at[d, c], "dp", peer
        )

    def d_arrival(j, c):
        peer = lax.rem(d + j, n_dp)
        return remote(
            dsend.at[peer, c], din.at[peer, c], d_s.at[j, c], d_r.at[peer, c], "dp", peer
        )

    def y_copy(s, c):
        return remote(
            ysend.at[s, c], yin.at[t, c], y_s.at[s, c], y_r.at[t, c], "tensor", block_at(s)
        )

    def y_arrival(j, c):
        peer = lax.rem(t + j, n_t)
        return remote(
            ysend.at[0, c], yin.at[peer, c], y_s.at[0, c], y_r.at[peer, c], "tensor", peer
        )

    for j in range(n_dp - 1, 0, -1):
        msg_copy(j).start()

    def base_step(s, _):
        for c in range(nch):
            w_copy(s, c).wait()
            part = jnp.dot(att_ref[...], wbuf[s, c], preferred_element_type=F32)
            ysend[s, c] = part.astype(BF16)
            y_copy(s, c).start()

    first, second = (n_t - 1) // 2 + 1, n_t - 1
    first = min(first, second)
    lax.fori_loop(0, first, base_step, None)

    for j in range(1, n_dp):
        msg_arrival(j).wait_recv()
    down_copy.wait()
    got = msg_in[...].reshape(rows_c, depth + lanes)
    low = lax.dot_general(
        got[:, :depth], dbuf[...], (((1,), (1,)), ((), ())), preferred_element_type=F32
    )
    group = lax.broadcasted_iota(jnp.int32, (lanes, spread_w), 1) // rank
    index = lax.broadcasted_iota(jnp.int32, (lanes, spread_w), 0)
    expand = jnp.where(group == index, 1.0, 0.0).astype(BF16)
    mask[...] = jnp.dot(got[:, depth:], expand, preferred_element_type=F32)
    low = low * mask[...]
    folded = low[:, :lanes]
    for i in range(1, spread_w // lanes):
        folded = folded + low[:, i * lanes : (i + 1) * lanes]
    folded = folded + pltpu.roll(folded, rank, 1)
    left = lax.broadcasted_iota(jnp.int32, (half, lanes), 1) < rank
    low_own[...] = jnp.where(left, folded[:half], folded[half:])
    low_in[t] = low_own[...]
    for j in range(1, n_t):
        low_copy(j).start()

    lax.fori_loop(first, second, base_step, None)
    for c in range(nch):
        w_copy(n_t - 1, c).wait()
        own[c] = jnp.dot(att_ref[...], wbuf[n_t - 1, c], preferred_element_type=F32)

    for j in range(1, n_t):
        low_arrival(j).wait_recv()
    total = low_in[0]
    for i in range(1, n_t):
        total = total + low_in[i]
    turned = pltpu.roll(total, rank, 1)
    both = jnp.concatenate(
        [jnp.where(left, total, turned), jnp.where(left, turned, total)], axis=0
    )
    state = jnp.concatenate([both] * (spread_w // lanes), axis=1)
    spread = (state * mask[...]).astype(BF16)
    up_copy.wait()
    for c in range(nch):
        delta = jnp.dot(
            spread, ubuf[:, c * chunk : (c + 1) * chunk], preferred_element_type=F32
        )
        dsend[:, c] = delta.astype(BF16).reshape(n_dp, cap, chunk)
        din[d, c] = dsend[d, c]
        for j in range(n_dp - 1, 0, -1):
            d_copy(j, c).start()

    for c in range(nch):
        total = own[c]
        for j in range(1, n_t):
            y_arrival(j, c).wait_recv()
            total = total + yin[lax.rem(t + j, n_t), c].astype(F32)
        for j in range(1, n_dp):
            d_arrival(j, c).wait_recv()
        delta = lax.dot_general(
            sel_ref[...], din[:, c].reshape(rows_c, chunk), (((0,), (0,)), ((), ())),
            preferred_element_type=F32,
        )
        out_ref[:, c * chunk : (c + 1) * chunk] = (total + delta).astype(BF16)

    for j in range(1, n_dp):
        msg_copy(j).wait_send()
        for c in range(nch):
            d_copy(j, c).wait_send()
    for j in range(1, n_t):
        low_copy(j).wait_send()

    def drain(s, _):
        for c in range(nch):
            y_copy(s, c).wait_send()

    lax.fori_loop(0, n_t - 1, drain, None)


def local(
    n_dp, n_t, attended, output_weight, down_factor_table, up_factor_table,
    request_adapter_index, adapter_row_table,
):
    rows, depth = attended.shape
    adapters, _, rank = down_factor_table.shape
    columns = output_weight.shape[1] // n_t
    chunk = min(512, columns)
    nch = columns // chunk
    cap = 2 * rows // n_dp
    lanes = 2 * rank
    spread_w = adapters * rank

    table_len = adapter_row_table.shape[0]
    match = request_adapter_index[:, None] == jnp.arange(table_len, dtype=jnp.int32)[None, :]
    row_of = jnp.sum(jnp.where(match, adapter_row_table[None, :], 0), axis=1)
    owner, held = row_of // adapters, row_of % adapters
    earlier = jnp.arange(rows)[None, :] < jnp.arange(rows)[:, None]
    place = jnp.sum((owner[:, None] == owner[None, :]) & earlier, axis=1, dtype=jnp.int32)
    slot = owner * cap + place
    sel = (jnp.arange(n_dp * cap, dtype=jnp.int32)[:, None] == slot[None, :]).astype(BF16)
    loc = (held[:, None] == jnp.arange(lanes, dtype=jnp.int32)[None, :]).astype(BF16)
    down = jnp.swapaxes(down_factor_table, 1, 2).reshape(spread_w, depth)
    up = up_factor_table.reshape(spread_w, columns)

    vmem, anywhere = pl.BlockSpec(memory_space=pltpu.VMEM), pl.BlockSpec(memory_space=pl.ANY)
    dma = pltpu.SemaphoreType.DMA
    return pl.pallas_call(
        functools.partial(kernel, n_dp, n_t),
        out_shape=jax.ShapeDtypeStruct((rows, columns), BF16),
        in_specs=[vmem] * 3 + [anywhere] * 3,
        out_specs=vmem,
        scratch_shapes=[
            pltpu.VMEM((n_t, nch, depth, chunk), BF16),
            pltpu.VMEM((spread_w, depth), BF16),
            pltpu.VMEM((spread_w, columns), BF16),
            pltpu.VMEM((n_dp, cap, depth + lanes), BF16),
            pltpu.VMEM((n_dp, cap, depth + lanes), BF16),
            pltpu.VMEM((n_dp * cap, spread_w), F32),
            pltpu.VMEM((n_dp * cap // 2, lanes), F32),
            pltpu.VMEM((n_t, n_dp * cap // 2, lanes), F32),
            pltpu.VMEM((n_dp, nch, cap, chunk), BF16),
            pltpu.VMEM((n_dp, nch, cap, chunk), BF16),
            pltpu.VMEM((n_t, nch, rows, chunk), BF16),
            pltpu.VMEM((n_t, nch, rows, chunk), BF16),
            pltpu.VMEM((nch, rows, chunk), F32),
            dma((n_t, nch)),
            dma((2,)),
            dma((n_dp,)),
            dma((n_dp,)),
            dma((n_t,)),
            dma((n_t,)),
            dma((n_dp, nch)),
            dma((n_dp, nch)),
            dma((n_t, nch)),
            dma((n_t, nch)),
        ],
        compiler_params=pltpu.CompilerParams(
            collective_id=0, has_side_effects=True, vmem_limit_bytes=56 * 1024 * 1024
        ),
    )(attended, sel, loc, output_weight, down, up)


def solution(mesh):
    in_specs = (
        P(("groups", "dp"), "tensor"),
        P("tensor", None),
        P("dp", "tensor", None),
        P("dp", None, "tensor"),
        P(("groups", "dp")),
        P("groups"),
    )
    out_specs = P(("groups", "dp"), "tensor")
    body = functools.partial(local, mesh.shape["dp"], mesh.shape["tensor"])
    return jax.shard_map(body, mesh=mesh, in_specs=in_specs, out_specs=out_specs, check_vma=False)
```

```python
import functools

import jax
import jax.numpy as jnp
from jax import lax
from jax.experimental import pallas as pl
from jax.experimental.pallas import tpu as pltpu
from jax.sharding import PartitionSpec as P

MESH = pl.DeviceIdType.MESH
F32, BF16 = jnp.float32, jnp.bfloat16


def kernel(
    n_dp, n_t, adapters, att_hbm, idx_ref, tab_ref, w_ref, down_ref, up_ref, out_ref,
    att_ref, wbuf, dbuf, ubuf, sel_ref, msg, msg_in, mask, low_own, low_in, dsend, din,
    ysend, yin, own, w_sem, ad_sem, msg_s, msg_r, low_s, low_r, d_s, d_r, y_s, y_r,
):
    d, t = lax.axis_index("dp"), lax.axis_index("tensor")
    rows, depth = att_ref.shape
    nch, chunk = wbuf.shape[1], wbuf.shape[3]
    width = nch * chunk
    cap = msg.shape[1]
    rows_c = n_dp * cap
    half = rows_c // 2
    lanes = low_own.shape[1]
    rank = lanes // 2
    spread_w = dbuf.shape[0]
    steps = (n_t - 1) * nch
    edge = jnp.logical_or(t == 0, t == n_t - 1)

    barrier = pltpu.get_barrier_semaphore()
    for j in range(1, n_dp):
        pl.semaphore_signal(
            barrier, inc=1, device_id={"dp": lax.rem(d + j, n_dp)}, device_id_type=MESH
        )
    for j in range(1, n_t):
        pl.semaphore_signal(
            barrier, inc=1, device_id={"tensor": lax.rem(t + j, n_t)}, device_id_type=MESH
        )

    to_left, to_right = t, n_t - 1 - t
    shorter = jnp.minimum(to_left, to_right)
    right_longer = to_right >= to_left

    def block_at(s):
        in_turn = s < 2 * shorter
        k = jnp.where(in_turn, s // 2, s - shorter)
        even = lax.rem(s, 2) == 0
        right = jnp.logical_xor(jnp.logical_and(in_turn, jnp.logical_not(even)), right_longer)
        return jnp.where(s == n_t - 1, t, jnp.where(right, n_t - 1 - k, k))

    def w_copy(s, c):
        start = pl.multiple_of(block_at(s) * width + c * chunk, chunk)
        return pltpu.make_async_copy(
            w_ref.at[:, pl.ds(start, chunk)], wbuf.at[s, c], w_sem.at[s, c]
        )

    def fetch(s, _):
        for c in range(nch):
            w_copy(s, c).start()

    att_copy = pltpu.make_async_copy(att_hbm, att_ref, ad_sem.at[2])
    down_copy = pltpu.make_async_copy(down_ref, dbuf, ad_sem.at[0])
    up_copy = pltpu.make_async_copy(up_ref, ubuf, ad_sem.at[1])
    att_copy.start()
    early = max(n_t // 2, 1)
    fetch(0, None)
    down_copy.start()
    lax.fori_loop(1, early, fetch, None)
    up_copy.start()
    lax.fori_loop(early, n_t, fetch, None)

    @pl.when(t == 0)
    def _():
        yin[:n_t] = jnp.zeros((n_t,) + yin.shape[1:], BF16)

    @pl.when(t == n_t - 1)
    def _():
        yin[: n_t - 1] = jnp.zeros((n_t - 1,) + yin.shape[1:], BF16)
        yin[n_t] = jnp.zeros(yin.shape[1:], BF16)

    def iota(shape, axis):
        return lax.broadcasted_iota(jnp.int32, shape, axis)

    def flag(condition):
        return jnp.where(condition, 1.0, 0.0)

    table_len = tab_ref.shape[1]
    asked = flag(idx_ref[...] == iota((table_len, rows), 0)).astype(BF16)
    table = jnp.broadcast_to(tab_ref[...].astype(F32), (8, table_len)).astype(BF16)
    row_of = jnp.dot(table, asked, preferred_element_type=F32)[:1].astype(jnp.int32)
    group = iota((n_dp, rows), 0)
    owned = flag((row_of >= group * adapters) & (row_of < (group + 1) * adapters))
    earlier = flag(iota((rows, rows), 0) < iota((rows, rows), 1)).astype(BF16)
    place = jnp.dot(owned.astype(BF16), earlier, preferred_element_type=F32)
    group = group.astype(F32)
    slot = jnp.sum(owned * (group * cap + place), axis=0, keepdims=True).astype(jnp.int32)
    held = row_of - jnp.sum(owned * group * adapters, axis=0, keepdims=True).astype(jnp.int32)
    sel_ref[...] = flag(iota((rows_c, rows), 0) == slot).astype(BF16)
    held_at = flag(iota((lanes, rows), 0) == held).astype(BF16)
    picks = lax.dot_general(
        sel_ref[...], held_at, (((1,), (1,)), ((), ())), preferred_element_type=F32
    )
    msg[:, :, depth:] = picks.astype(BF16).reshape(n_dp, cap, lanes)
    att_copy.wait()
    rows_of = jnp.dot(sel_ref[...], att_ref[...], preferred_element_type=F32)
    msg[:, :, :depth] = rows_of.astype(BF16).reshape(n_dp, cap, depth)
    pl.semaphore_wait(barrier, n_dp - 1 + n_t - 1)

    def remote(src, dst, send, recv, axis, peer):
        return pltpu.make_async_remote_copy(
            src_ref=src, dst_ref=dst, send_sem=send, recv_sem=recv,
            device_id={axis: peer}, device_id_type=MESH,
        )

    def msg_copy(j):
        peer = lax.rem(d + j, n_dp)
        return remote(msg.at[peer], msg_in.at[d], msg_s.at[j], msg_r.at[d], "dp", peer)

    def msg_arrival(j):
        peer = lax.rem(d + j, n_dp)
        return remote(msg.at[peer], msg_in.at[peer], msg_s.at[j], msg_r.at[peer], "dp", peer)

    def low_copy(j):
        peer = lax.rem(t + j, n_t)
        return remote(low_own, low_in.at[t], low_s.at[j], low_r.at[t], "tensor", peer)

    def low_arrival(j):
        peer = lax.rem(t + j, n_t)
        return remote(low_own, low_in.at[peer], low_s.at[j], low_r.at[peer], "tensor", peer)

    def d_copy(j, c):
        peer = lax.rem(d + j, n_dp)
        return remote(
            dsend.at[peer, c], din.at[d, c], d_s.at[j, c], d_r.at[d, c], "dp", peer
        )

    def d_arrival(j, c):
        peer = lax.rem(d + j, n_dp)
        return remote(
            dsend.at[peer, c], din.at[peer, c], d_s.at[j, c], d_r.at[peer, c], "dp", peer
        )

    def y_copy(s, c):
        b = block_at(s)
        right = b > t
        peer = jnp.where(right, t + 1, t - 1)
        at = jnp.where(jnp.logical_and(b == peer, jnp.logical_not(right)), n_t, b)
        return remote(
            ysend.at[s, c], yin.at[at, c], y_s.at[s, c], y_r.at[at, c], "tensor", peer
        )

    def y_arrival(at, c):
        return remote(
            ysend.at[0, c], yin.at[at, c], y_s.at[0, c], y_r.at[at, c], "tensor",
            jnp.where(t > 0, t - 1, t + 1),
        )

    for j in range(n_dp - 1, 0, -1):
        msg_copy(j).start()
    msg_in[d] = msg[d]

    def base_step(q, _):
        s, c = q // nch, lax.rem(q, nch)
        w_copy(s, c).wait()
        part = jnp.dot(att_ref[...], wbuf[s, c], preferred_element_type=F32)
        b = block_at(s)

        @pl.when(jnp.logical_not(edge))
        def _():
            y_arrival(b, c).wait_recv()

        ysend[s, c] = (part + yin[b, c].astype(F32)).astype(BF16)
        y_copy(s, c).start()

    first = jnp.where(edge, max(steps // 2, 1), max((steps * 5) // 12, 1))
    lax.fori_loop(0, first, base_step, None)

    for j in range(1, n_dp):
        msg_arrival(j).wait_recv()
    down_copy.wait()
    got = msg_in[...].reshape(rows_c, depth + lanes)
    low = lax.dot_general(
        got[:, :depth], dbuf[...], (((1,), (1,)), ((), ())), preferred_element_type=F32
    )
    expand = flag(iota((lanes, spread_w), 1) // rank == iota((lanes, spread_w), 0)).astype(BF16)
    mask[...] = jnp.dot(got[:, depth:], expand, preferred_element_type=F32)
    low = low * mask[...]
    folded = low[:, :lanes]
    for i in range(1, spread_w // lanes):
        folded = folded + low[:, i * lanes : (i + 1) * lanes]
    folded = folded + pltpu.roll(folded, rank, 1)
    left = iota((half, lanes), 1) < rank
    low_own[...] = jnp.where(left, folded[:half], folded[half:]).astype(BF16)
    low_in[t] = low_own[...]
    for j in range(1, n_t):
        low_copy(j).start()

    lax.fori_loop(first, steps, base_step, None)
    for c in range(nch):
        w_copy(n_t - 1, c).wait()
        own[c] = jnp.dot(att_ref[...], wbuf[n_t - 1, c], preferred_element_type=F32)

    for j in range(1, n_t):
        low_arrival(j).wait_recv()
    total = low_in[0].astype(F32)
    for i in range(1, n_t):
        total = total + low_in[i].astype(F32)
    turned = pltpu.roll(total, rank, 1)
    both = jnp.concatenate(
        [jnp.where(left, total, turned), jnp.where(left, turned, total)], axis=0
    )
    state = jnp.concatenate([both] * (spread_w // lanes), axis=1)
    spread = (state * mask[...]).astype(BF16)
    up_copy.wait()
    for c in range(nch):
        delta = jnp.dot(
            spread, ubuf[:, c * chunk : (c + 1) * chunk], preferred_element_type=F32
        )
        dsend[:, c] = delta.astype(BF16).reshape(n_dp, cap, chunk)
        for j in range(n_dp - 1, 0, -1):
            d_copy(j, c).start()
        din[d, c] = dsend[d, c]

    for c in range(nch):
        @pl.when(t > 0)
        def _():
            y_arrival(t, c).wait_recv()

        @pl.when(t < n_t - 1)
        def _():
            y_arrival(n_t, c).wait_recv()

        base = own[c] + yin[t, c].astype(F32) + yin[n_t, c].astype(F32)
        for j in range(1, n_dp):
            d_arrival(j, c).wait_recv()
        delta = lax.dot_general(
            sel_ref[...], din[:, c].reshape(rows_c, chunk), (((0,), (0,)), ((), ())),
            preferred_element_type=F32,
        )
        out_ref[:, c * chunk : (c + 1) * chunk] = (base + delta).astype(BF16)

    for j in range(1, n_dp):
        msg_copy(j).wait_send()
        for c in range(nch):
            d_copy(j, c).wait_send()
    for j in range(1, n_t):
        low_copy(j).wait_send()

    def drain(s, _):
        for c in range(nch):
            y_copy(s, c).wait_send()

    lax.fori_loop(0, n_t - 1, drain, None)


def local(
    n_dp, n_t, attended, output_weight, down_factor_table, up_factor_table,
    request_adapter_index, adapter_row_table,
):
    rows, depth = attended.shape
    adapters, _, rank = down_factor_table.shape
    columns = output_weight.shape[1] // n_t
    chunk = min(512, columns)
    nch = columns // chunk
    cap = 2 * rows // n_dp
    lanes = 2 * rank
    spread_w = adapters * rank

    down = jnp.swapaxes(down_factor_table, 1, 2).reshape(spread_w, depth)
    up = up_factor_table.reshape(spread_w, columns)

    vmem, anywhere = pl.BlockSpec(memory_space=pltpu.VMEM), pl.BlockSpec(memory_space=pl.ANY)
    dma = pltpu.SemaphoreType.DMA
    return pl.pallas_call(
        functools.partial(kernel, n_dp, n_t, adapters),
        out_shape=jax.ShapeDtypeStruct((rows, columns), BF16),
        in_specs=[anywhere, vmem, vmem] + [anywhere] * 3,
        out_specs=vmem,
        scratch_shapes=[
            pltpu.VMEM((rows, depth), BF16),
            pltpu.VMEM((n_t, nch, depth, chunk), BF16),
            pltpu.VMEM((spread_w, depth), BF16),
            pltpu.VMEM((spread_w, columns), BF16),
            pltpu.VMEM((n_dp * cap, rows), BF16),
            pltpu.VMEM((n_dp, cap, depth + lanes), BF16),
            pltpu.VMEM((n_dp, cap, depth + lanes), BF16),
            pltpu.VMEM((n_dp * cap, spread_w), F32),
            pltpu.VMEM((n_dp * cap // 2, lanes), BF16),
            pltpu.VMEM((n_t, n_dp * cap // 2, lanes), BF16),
            pltpu.VMEM((n_dp, nch, cap, chunk), BF16),
            pltpu.VMEM((n_dp, nch, cap, chunk), BF16),
            pltpu.VMEM((n_t, nch, rows, chunk), BF16),
            pltpu.VMEM((n_t + 1, nch, rows, chunk), BF16),
            pltpu.VMEM((nch, rows, chunk), F32),
            dma((n_t, nch)),
            dma((3,)),
            dma((n_dp,)),
            dma((n_dp,)),
            dma((n_t,)),
            dma((n_t,)),
            dma((n_dp, nch)),
            dma((n_dp, nch)),
            dma((n_t, nch)),
            dma((n_t + 1, nch)),
        ],
        compiler_params=pltpu.CompilerParams(
            collective_id=0, has_side_effects=True, vmem_limit_bytes=56 * 1024 * 1024
        ),
    )(attended, request_adapter_index[None, :], adapter_row_table[None, :], output_weight, down, up)


def solution(mesh):
    in_specs = (
        P(("groups", "dp"), "tensor"),
        P("tensor", None),
        P("dp", "tensor", None),
        P("dp", None, "tensor"),
        P(("groups", "dp")),
        P("groups"),
    )
    out_specs = P(("groups", "dp"), "tensor")
    body = functools.partial(local, mesh.shape["dp"], mesh.shape["tensor"])
    return jax.shard_map(body, mesh=mesh, in_specs=in_specs, out_specs=out_specs, check_vma=False)
```

```python
import functools

import jax
import jax.numpy as jnp
from jax import lax
from jax.experimental import pallas as pl
from jax.experimental.pallas import tpu as pltpu
from jax.sharding import PartitionSpec as P

MESH = pl.DeviceIdType.MESH
F32, BF16 = jnp.float32, jnp.bfloat16


def kernel(
    n_dp, n_t, adapters, att_hbm, idx_ref, tab_ref, w_ref, down_ref, up_ref, out_ref,
    att_ref, wbuf, dbuf, ubuf, sel_ref, msg, msg_in, mask, low_own, low_in, dsend, din,
    ysend, yin, own, w_sem, ad_sem, msg_s, msg_r, low_s, low_r, d_s, d_r, y_s, y_r,
):
    d, t = lax.axis_index("dp"), lax.axis_index("tensor")
    rows, depth = att_ref.shape
    nch, chunk = wbuf.shape[1], wbuf.shape[3]
    width = nch * chunk
    cap = msg.shape[1]
    rows_c = n_dp * cap
    half = rows_c // 2
    lanes = low_own.shape[1]
    rank = lanes // 2
    spread_w = dbuf.shape[0]
    steps = (n_t - 1) * nch
    edge = jnp.logical_or(t == 0, t == n_t - 1)

    barrier = pltpu.get_barrier_semaphore()
    for j in range(1, n_dp):
        pl.semaphore_signal(
            barrier, inc=1, device_id={"dp": lax.rem(d + j, n_dp)}, device_id_type=MESH
        )
    for j in range(1, n_t):
        pl.semaphore_signal(
            barrier, inc=1, device_id={"tensor": lax.rem(t + j, n_t)}, device_id_type=MESH
        )

    to_left, to_right = t, n_t - 1 - t
    shorter = jnp.minimum(to_left, to_right)
    right_longer = to_right >= to_left

    def block_at(s):
        in_turn = s < 2 * shorter
        k = jnp.where(in_turn, s // 2, s - shorter)
        even = lax.rem(s, 2) == 0
        right = jnp.logical_xor(jnp.logical_and(in_turn, jnp.logical_not(even)), right_longer)
        return jnp.where(s == n_t - 1, t, jnp.where(right, n_t - 1 - k, k))

    def w_copy(s, c):
        start = pl.multiple_of(block_at(s) * width + c * chunk, chunk)
        return pltpu.make_async_copy(
            w_ref.at[:, pl.ds(start, chunk)], wbuf.at[s, c], w_sem.at[s, c]
        )

    ahead = min(3, n_t * nch)

    def fetch(q):
        w_copy(q // nch, lax.rem(q, nch)).start()

    att_copy = pltpu.make_async_copy(att_hbm, att_ref, ad_sem.at[2])
    down_copy = pltpu.make_async_copy(down_ref, dbuf, ad_sem.at[0])
    up_copy = pltpu.make_async_copy(up_ref, ubuf, ad_sem.at[1])
    att_copy.start()
    for q in range(ahead):
        fetch(jnp.int32(q))
    down_copy.start()

    @pl.when(t == 0)
    def _():
        yin[:n_t] = jnp.zeros((n_t,) + yin.shape[1:], BF16)

    @pl.when(t == n_t - 1)
    def _():
        yin[: n_t - 1] = jnp.zeros((n_t - 1,) + yin.shape[1:], BF16)
        yin[n_t] = jnp.zeros(yin.shape[1:], BF16)

    def iota(shape, axis):
        return lax.broadcasted_iota(jnp.int32, shape, axis)

    def flag(condition):
        return jnp.where(condition, 1.0, 0.0)

    table_len = tab_ref.shape[1]
    asked = flag(idx_ref[...] == iota((table_len, rows), 0)).astype(BF16)
    table = jnp.broadcast_to(tab_ref[...].astype(F32), (8, table_len)).astype(BF16)
    row_of = jnp.dot(table, asked, preferred_element_type=F32)[:1].astype(jnp.int32)
    group = iota((n_dp, rows), 0)
    owned = flag((row_of >= group * adapters) & (row_of < (group + 1) * adapters))
    earlier = flag(iota((rows, rows), 0) < iota((rows, rows), 1)).astype(BF16)
    place = jnp.dot(owned.astype(BF16), earlier, preferred_element_type=F32)
    group = group.astype(F32)
    slot = jnp.sum(owned * (group * cap + place), axis=0, keepdims=True).astype(jnp.int32)
    held = row_of - jnp.sum(owned * group * adapters, axis=0, keepdims=True).astype(jnp.int32)
    sel_ref[...] = flag(iota((rows_c, rows), 0) == slot).astype(BF16)
    held_at = flag(iota((lanes, rows), 0) == held).astype(BF16)
    picks = lax.dot_general(
        sel_ref[...], held_at, (((1,), (1,)), ((), ())), preferred_element_type=F32
    )
    msg[:, :, depth:] = picks.astype(BF16).reshape(n_dp, cap, lanes)
    att_copy.wait()
    rows_of = jnp.dot(sel_ref[...], att_ref[...], preferred_element_type=F32)
    msg[:, :, :depth] = rows_of.astype(BF16).reshape(n_dp, cap, depth)
    pl.semaphore_wait(barrier, n_dp - 1 + n_t - 1)

    def remote(src, dst, send, recv, axis, peer):
        return pltpu.make_async_remote_copy(
            src_ref=src, dst_ref=dst, send_sem=send, recv_sem=recv,
            device_id={axis: peer}, device_id_type=MESH,
        )

    def msg_copy(j):
        peer = lax.rem(d + j, n_dp)
        return remote(msg.at[peer], msg_in.at[d], msg_s.at[j], msg_r.at[d], "dp", peer)

    def msg_arrival(j):
        peer = lax.rem(d + j, n_dp)
        return remote(msg.at[peer], msg_in.at[peer], msg_s.at[j], msg_r.at[peer], "dp", peer)

    def low_copy(j):
        peer = lax.rem(t + j, n_t)
        return remote(low_own, low_in.at[t], low_s.at[j], low_r.at[t], "tensor", peer)

    def low_arrival(j):
        peer = lax.rem(t + j, n_t)
        return remote(low_own, low_in.at[peer], low_s.at[j], low_r.at[peer], "tensor", peer)

    def d_copy(j, c):
        peer = lax.rem(d + j, n_dp)
        return remote(
            dsend.at[peer, c], din.at[d, c], d_s.at[j, c], d_r.at[d, c], "dp", peer
        )

    def d_arrival(j, c):
        peer = lax.rem(d + j, n_dp)
        return remote(
            dsend.at[peer, c], din.at[peer, c], d_s.at[j, c], d_r.at[peer, c], "dp", peer
        )

    def y_copy(s, c):
        b = block_at(s)
        right = b > t
        peer = jnp.where(right, t + 1, t - 1)
        at = jnp.where(jnp.logical_and(b == peer, jnp.logical_not(right)), n_t, b)
        return remote(
            ysend.at[s, c], yin.at[at, c], y_s.at[s, c], y_r.at[at, c], "tensor", peer
        )

    def y_arrival(at, c):
        return remote(
            ysend.at[0, c], yin.at[at, c], y_s.at[0, c], y_r.at[at, c], "tensor",
            jnp.where(t > 0, t - 1, t + 1),
        )

    for j in range(n_dp - 1, 0, -1):
        msg_copy(j).start()
    msg_in[d] = msg[d]

    def base_step(q, _):
        s, c = q // nch, lax.rem(q, nch)
        w_copy(s, c).wait()

        @pl.when(q + ahead < n_t * nch)
        def _():
            fetch(q + ahead)

        part = jnp.dot(att_ref[...], wbuf[s, c], preferred_element_type=F32)
        b = block_at(s)

        @pl.when(jnp.logical_not(edge))
        def _():
            y_arrival(b, c).wait_recv()

        ysend[s, c] = (part + yin[b, c].astype(F32)).astype(BF16)
        y_copy(s, c).start()

    first = jnp.where(edge, max(steps * 6 // 12, 1), max(steps * 4 // 12, 1))
    second = jnp.where(edge, max(steps * 10 // 12, 1), max(steps * 9 // 12, 1))
    lax.fori_loop(0, first, base_step, None)
    up_copy.start()

    for j in range(1, n_dp):
        msg_arrival(j).wait_recv()
    down_copy.wait()
    got = msg_in[...].reshape(rows_c, depth + lanes)
    low = lax.dot_general(
        got[:, :depth], dbuf[...], (((1,), (1,)), ((), ())), preferred_element_type=F32
    )
    expand = flag(iota((lanes, spread_w), 1) // rank == iota((lanes, spread_w), 0)).astype(BF16)
    mask[...] = jnp.dot(got[:, depth:], expand, preferred_element_type=F32)
    low = low * mask[...]
    folded = low[:, :lanes]
    for i in range(1, spread_w // lanes):
        folded = folded + low[:, i * lanes : (i + 1) * lanes]
    folded = folded + pltpu.roll(folded, rank, 1)
    left = iota((half, lanes), 1) < rank
    low_own[...] = jnp.where(left, folded[:half], folded[half:]).astype(BF16)
    low_in[t] = low_own[...]
    for j in range(1, n_t):
        low_copy(j).start()

    lax.fori_loop(first, second, base_step, None)
    for j in range(1, n_t):
        low_arrival(j).wait_recv()
    total = low_in[0].astype(F32)
    for i in range(1, n_t):
        total = total + low_in[i].astype(F32)
    turned = pltpu.roll(total, rank, 1)
    both = jnp.concatenate(
        [jnp.where(left, total, turned), jnp.where(left, turned, total)], axis=0
    )
    state = jnp.concatenate([both] * (spread_w // lanes), axis=1)
    spread = (state * mask[...]).astype(BF16)
    up_copy.wait()
    for c in range(nch):
        delta = jnp.dot(
            spread, ubuf[:, c * chunk : (c + 1) * chunk], preferred_element_type=F32
        )
        dsend[:, c] = delta.astype(BF16).reshape(n_dp, cap, chunk)
        for j in range(n_dp - 1, 0, -1):
            d_copy(j, c).start()
        din[d, c] = dsend[d, c]

    lax.fori_loop(second, steps, base_step, None)
    for c in range(nch):
        w_copy(n_t - 1, c).wait()
        if steps + c + ahead < n_t * nch:
            fetch(jnp.int32(steps + c + ahead))
        own[c] = jnp.dot(att_ref[...], wbuf[n_t - 1, c], preferred_element_type=F32)

    for c in range(nch):
        @pl.when(t > 0)
        def _():
            y_arrival(t, c).wait_recv()

        @pl.when(t < n_t - 1)
        def _():
            y_arrival(n_t, c).wait_recv()

        base = own[c] + yin[t, c].astype(F32) + yin[n_t, c].astype(F32)
        for j in range(1, n_dp):
            d_arrival(j, c).wait_recv()
        delta = lax.dot_general(
            sel_ref[...], din[:, c].reshape(rows_c, chunk), (((0,), (0,)), ((), ())),
            preferred_element_type=F32,
        )
        out_ref[:, c * chunk : (c + 1) * chunk] = (base + delta).astype(BF16)

    for j in range(1, n_dp):
        msg_copy(j).wait_send()
        for c in range(nch):
            d_copy(j, c).wait_send()
    for j in range(1, n_t):
        low_copy(j).wait_send()

    def drain(s, _):
        for c in range(nch):
            y_copy(s, c).wait_send()

    lax.fori_loop(0, n_t - 1, drain, None)


def local(
    n_dp, n_t, attended, output_weight, down_factor_table, up_factor_table,
    request_adapter_index, adapter_row_table,
):
    rows, depth = attended.shape
    adapters, _, rank = down_factor_table.shape
    columns = output_weight.shape[1] // n_t
    chunk = min(512, columns)
    nch = columns // chunk
    cap = 2 * rows // n_dp
    lanes = 2 * rank
    spread_w = adapters * rank

    down = jnp.swapaxes(down_factor_table, 1, 2).reshape(spread_w, depth)
    up = up_factor_table.reshape(spread_w, columns)

    vmem, anywhere = pl.BlockSpec(memory_space=pltpu.VMEM), pl.BlockSpec(memory_space=pl.ANY)
    dma = pltpu.SemaphoreType.DMA
    return pl.pallas_call(
        functools.partial(kernel, n_dp, n_t, adapters),
        out_shape=pltpu.VMEM((rows, columns), BF16),
        in_specs=[anywhere, vmem, vmem] + [anywhere] * 3,
        out_specs=vmem,
        scratch_shapes=[
            pltpu.VMEM((rows, depth), BF16),
            pltpu.VMEM((n_t, nch, depth, chunk), BF16),
            pltpu.VMEM((spread_w, depth), BF16),
            pltpu.VMEM((spread_w, columns), BF16),
            pltpu.VMEM((n_dp * cap, rows), BF16),
            pltpu.VMEM((n_dp, cap, depth + lanes), BF16),
            pltpu.VMEM((n_dp, cap, depth + lanes), BF16),
            pltpu.VMEM((n_dp * cap, spread_w), F32),
            pltpu.VMEM((n_dp * cap // 2, lanes), BF16),
            pltpu.VMEM((n_t, n_dp * cap // 2, lanes), BF16),
            pltpu.VMEM((n_dp, nch, cap, chunk), BF16),
            pltpu.VMEM((n_dp, nch, cap, chunk), BF16),
            pltpu.VMEM((n_t, nch, rows, chunk), BF16),
            pltpu.VMEM((n_t + 1, nch, rows, chunk), BF16),
            pltpu.VMEM((nch, rows, chunk), F32),
            dma((n_t, nch)),
            dma((3,)),
            dma((n_dp,)),
            dma((n_dp,)),
            dma((n_t,)),
            dma((n_t,)),
            dma((n_dp, nch)),
            dma((n_dp, nch)),
            dma((n_t, nch)),
            dma((n_t + 1, nch)),
        ],
        compiler_params=pltpu.CompilerParams(
            collective_id=0, has_side_effects=True, vmem_limit_bytes=56 * 1024 * 1024
        ),
    )(attended, request_adapter_index[None, :], adapter_row_table[None, :], output_weight, down, up)


def solution(mesh):
    in_specs = (
        P(("groups", "dp"), "tensor"),
        P("tensor", None),
        P("dp", "tensor", None),
        P("dp", None, "tensor"),
        P(("groups", "dp")),
        P("groups"),
    )
    out_specs = P(("groups", "dp"), "tensor")
    body = functools.partial(local, mesh.shape["dp"], mesh.shape["tensor"])
    return jax.shard_map(body, mesh=mesh, in_specs=in_specs, out_specs=out_specs, check_vma=False)
```

```python
import functools

import jax
import jax.numpy as jnp
from jax import lax
from jax.experimental import pallas as pl
from jax.experimental.pallas import tpu as pltpu
from jax.sharding import PartitionSpec as P

MESH = pl.DeviceIdType.MESH
F32, BF16 = jnp.float32, jnp.bfloat16


def kernel(
    n_dp, n_t, adapters, att_hbm, idx_ref, tab_ref, w_ref, down_ref, up_ref, out_ref,
    att_ref, wbuf, dbuf, ubuf, sel_ref, msg, msg_in, mask, low_own, low_in, dsend, din,
    ysend, yin, own, w_sem, ad_sem, msg_s, msg_r, low_s, low_r, d_s, d_r, y_s, y_r,
):
    d, t = lax.axis_index("dp"), lax.axis_index("tensor")
    rows, depth = att_ref.shape
    nch, chunk = wbuf.shape[1], wbuf.shape[3]
    width = nch * chunk
    cap = msg.shape[1]
    rows_c = n_dp * cap
    half = rows_c // 2
    lanes = low_own.shape[1]
    rank = lanes // 2
    spread_w = dbuf.shape[0]
    steps = (n_t - 1) * nch
    edge = jnp.logical_or(t == 0, t == n_t - 1)

    barrier = pltpu.get_barrier_semaphore()
    for j in range(1, n_dp):
        pl.semaphore_signal(
            barrier, inc=1, device_id={"dp": lax.rem(d + j, n_dp)}, device_id_type=MESH
        )
    for j in range(1, n_t):
        pl.semaphore_signal(
            barrier, inc=1, device_id={"tensor": lax.rem(t + j, n_t)}, device_id_type=MESH
        )

    to_left, to_right = t, n_t - 1 - t
    shorter = jnp.minimum(to_left, to_right)
    right_longer = to_right >= to_left

    def block_at(s):
        in_turn = s < 2 * shorter
        k = jnp.where(in_turn, s // 2, s - shorter)
        even = lax.rem(s, 2) == 0
        right = jnp.logical_xor(jnp.logical_and(in_turn, jnp.logical_not(even)), right_longer)
        return jnp.where(s == n_t - 1, t, jnp.where(right, n_t - 1 - k, k))

    def w_copy(s, c):
        start = pl.multiple_of(block_at(s) * width + c * chunk, chunk)
        return pltpu.make_async_copy(
            w_ref.at[:, pl.ds(start, chunk)], wbuf.at[s, c], w_sem.at[s, c]
        )

    ahead = min(3, n_t * nch)

    def fetch(q):
        w_copy(q // nch, lax.rem(q, nch)).start()

    att_copy = pltpu.make_async_copy(att_hbm, att_ref, ad_sem.at[2])
    down_copy = pltpu.make_async_copy(down_ref, dbuf, ad_sem.at[0])
    up_copy = pltpu.make_async_copy(up_ref, ubuf, ad_sem.at[1])
    att_copy.start()
    for q in range(ahead):
        fetch(jnp.int32(q))
    down_copy.start()

    @pl.when(t == 0)
    def _():
        yin[:n_t] = jnp.zeros((n_t,) + yin.shape[1:], BF16)

    @pl.when(t == n_t - 1)
    def _():
        yin[: n_t - 1] = jnp.zeros((n_t - 1,) + yin.shape[1:], BF16)
        yin[n_t] = jnp.zeros(yin.shape[1:], BF16)

    def iota(shape, axis):
        return lax.broadcasted_iota(jnp.int32, shape, axis)

    def flag(condition):
        return jnp.where(condition, 1.0, 0.0)

    table_len = tab_ref.shape[1]
    asked = flag(idx_ref[...] == iota((table_len, rows), 0)).astype(BF16)
    table = jnp.broadcast_to(tab_ref[...].astype(F32), (8, table_len)).astype(BF16)
    row_of = jnp.dot(table, asked, preferred_element_type=F32)[:1].astype(jnp.int32)
    group = iota((n_dp, rows), 0)
    owned = flag((row_of >= group * adapters) & (row_of < (group + 1) * adapters))
    earlier = flag(iota((rows, rows), 0) < iota((rows, rows), 1)).astype(BF16)
    place = jnp.dot(owned.astype(BF16), earlier, preferred_element_type=F32)
    group = group.astype(F32)
    slot = jnp.sum(owned * (group * cap + place), axis=0, keepdims=True).astype(jnp.int32)
    held = row_of - jnp.sum(owned * group * adapters, axis=0, keepdims=True).astype(jnp.int32)
    sel_ref[...] = flag(iota((rows_c, rows), 0) == slot).astype(BF16)
    held_at = flag(iota((lanes, rows), 0) == held).astype(BF16)
    picks = lax.dot_general(
        sel_ref[...], held_at, (((1,), (1,)), ((), ())), preferred_element_type=F32
    )
    msg[:, :, depth:] = picks.astype(BF16).reshape(n_dp, cap, lanes)
    att_copy.wait()
    rows_of = jnp.dot(sel_ref[...], att_ref[...], preferred_element_type=F32)
    msg[:, :, :depth] = rows_of.astype(BF16).reshape(n_dp, cap, depth)
    pl.semaphore_wait(barrier, n_dp - 1 + n_t - 1)

    def remote(src, dst, send, recv, axis, peer):
        return pltpu.make_async_remote_copy(
            src_ref=src, dst_ref=dst, send_sem=send, recv_sem=recv,
            device_id={axis: peer}, device_id_type=MESH,
        )

    def msg_copy(j):
        peer = lax.rem(d + j, n_dp)
        return remote(msg.at[peer], msg_in.at[d], msg_s.at[j], msg_r.at[d], "dp", peer)

    def msg_arrival(j):
        peer = lax.rem(d + j, n_dp)
        return remote(msg.at[peer], msg_in.at[peer], msg_s.at[j], msg_r.at[peer], "dp", peer)

    def low_copy(j):
        peer = lax.rem(t + j, n_t)
        return remote(low_own, low_in.at[t], low_s.at[j], low_r.at[t], "tensor", peer)

    def low_arrival(j):
        peer = lax.rem(t + j, n_t)
        return remote(low_own, low_in.at[peer], low_s.at[j], low_r.at[peer], "tensor", peer)

    def d_copy(j, c):
        peer = lax.rem(d + j, n_dp)
        return remote(
            dsend.at[peer, c], din.at[d, c], d_s.at[j, c], d_r.at[d, c], "dp", peer
        )

    def d_arrival(j, c):
        peer = lax.rem(d + j, n_dp)
        return remote(
            dsend.at[peer, c], din.at[peer, c], d_s.at[j, c], d_r.at[peer, c], "dp", peer
        )

    def y_copy(s, c):
        b = block_at(s)
        right = b > t
        peer = jnp.where(right, t + 1, t - 1)
        at = jnp.where(jnp.logical_and(b == peer, jnp.logical_not(right)), n_t, b)
        return remote(
            ysend.at[s, c], yin.at[at, c], y_s.at[s, c], y_r.at[at, c], "tensor", peer
        )

    def y_arrival(at, c):
        return remote(
            ysend.at[0, c], yin.at[at, c], y_s.at[0, c], y_r.at[at, c], "tensor",
            jnp.where(t > 0, t - 1, t + 1),
        )

    for j in range(n_dp - 1, 0, -1):
        msg_copy(j).start()
    msg_in[d] = msg[d]

    def base_step(q, _):
        s, c = q // nch, lax.rem(q, nch)
        w_copy(s, c).wait()

        @pl.when(q + ahead < n_t * nch)
        def _():
            fetch(q + ahead)

        part = jnp.dot(att_ref[...], wbuf[s, c], preferred_element_type=F32)
        b = block_at(s)

        @pl.when(jnp.logical_not(edge))
        def _():
            y_arrival(b, c).wait_recv()

        ysend[s, c] = (part + yin[b, c].astype(F32)).astype(BF16)
        y_copy(s, c).start()

    first = jnp.where(edge, max(steps * 6 // 12, 1), max(steps * 3 // 12, 1))
    second = jnp.where(edge, max(steps * 10 // 12, 1), max(steps * 7 // 12, 1))
    lax.fori_loop(0, first, base_step, None)
    up_copy.start()

    for j in range(1, n_dp):
        msg_arrival(j).wait_recv()
    down_copy.wait()
    got = msg_in[...].reshape(rows_c, depth + lanes)
    low = lax.dot_general(
        got[:, :depth], dbuf[...], (((1,), (1,)), ((), ())), preferred_element_type=F32
    )
    expand = flag(iota((lanes, spread_w), 1) // rank == iota((lanes, spread_w), 0)).astype(BF16)
    mask[...] = jnp.dot(got[:, depth:], expand, preferred_element_type=F32)
    low = low * mask[...]
    folded = low[:, :lanes]
    for i in range(1, spread_w // lanes):
        folded = folded + low[:, i * lanes : (i + 1) * lanes]
    folded = folded + pltpu.roll(folded, rank, 1)
    left = iota((half, lanes), 1) < rank
    low_own[...] = jnp.where(left, folded[:half], folded[half:]).astype(BF16)
    low_in[t] = low_own[...]
    for j in range(1, n_t):
        low_copy(j).start()

    lax.fori_loop(first, second, base_step, None)
    for j in range(1, n_t):
        low_arrival(j).wait_recv()
    total = low_in[0].astype(F32)
    for i in range(1, n_t):
        total = total + low_in[i].astype(F32)
    turned = pltpu.roll(total, rank, 1)
    both = jnp.concatenate(
        [jnp.where(left, total, turned), jnp.where(left, turned, total)], axis=0
    )
    state = jnp.concatenate([both] * (spread_w // lanes), axis=1)
    spread = (state * mask[...]).astype(BF16)
    up_copy.wait()
    for c in range(nch):
        delta = jnp.dot(
            spread, ubuf[:, c * chunk : (c + 1) * chunk], preferred_element_type=F32
        )
        dsend[:, c] = delta.astype(BF16).reshape(n_dp, cap, chunk)
        for j in range(n_dp - 1, 0, -1):
            d_copy(j, c).start()
        din[d, c] = dsend[d, c]

    lax.fori_loop(second, steps, base_step, None)
    for c in range(nch):
        w_copy(n_t - 1, c).wait()
        if steps + c + ahead < n_t * nch:
            fetch(jnp.int32(steps + c + ahead))
        own[c] = jnp.dot(att_ref[...], wbuf[n_t - 1, c], preferred_element_type=F32)

    for c in range(nch):
        @pl.when(t > 0)
        def _():
            y_arrival(t, c).wait_recv()

        @pl.when(t < n_t - 1)
        def _():
            y_arrival(n_t, c).wait_recv()

        base = own[c] + yin[t, c].astype(F32) + yin[n_t, c].astype(F32)
        for j in range(1, n_dp):
            d_arrival(j, c).wait_recv()
        delta = lax.dot_general(
            sel_ref[...], din[:, c].reshape(rows_c, chunk), (((0,), (0,)), ((), ())),
            preferred_element_type=F32,
        )
        out_ref[:, c * chunk : (c + 1) * chunk] = (base + delta).astype(BF16)

    for j in range(1, n_dp):
        msg_copy(j).wait_send()
        for c in range(nch):
            d_copy(j, c).wait_send()
    for j in range(1, n_t):
        low_copy(j).wait_send()

    def drain(s, _):
        for c in range(nch):
            y_copy(s, c).wait_send()

    lax.fori_loop(0, n_t - 1, drain, None)


def local(
    n_dp, n_t, attended, output_weight, down_factor_table, up_factor_table,
    request_adapter_index, adapter_row_table,
):
    rows, depth = attended.shape
    adapters, _, rank = down_factor_table.shape
    columns = output_weight.shape[1] // n_t
    chunk = min(512, columns)
    nch = columns // chunk
    cap = 2 * rows // n_dp
    lanes = 2 * rank
    spread_w = adapters * rank

    down = jnp.swapaxes(down_factor_table, 1, 2).reshape(spread_w, depth)
    up = up_factor_table.reshape(spread_w, columns)

    vmem, anywhere = pl.BlockSpec(memory_space=pltpu.VMEM), pl.BlockSpec(memory_space=pl.ANY)
    dma = pltpu.SemaphoreType.DMA
    return pl.pallas_call(
        functools.partial(kernel, n_dp, n_t, adapters),
        out_shape=pltpu.VMEM((rows, columns), BF16),
        in_specs=[anywhere, vmem, vmem] + [anywhere] * 3,
        out_specs=vmem,
        scratch_shapes=[
            pltpu.VMEM((rows, depth), BF16),
            pltpu.VMEM((n_t, nch, depth, chunk), BF16),
            pltpu.VMEM((spread_w, depth), BF16),
            pltpu.VMEM((spread_w, columns), BF16),
            pltpu.VMEM((n_dp * cap, rows), BF16),
            pltpu.VMEM((n_dp, cap, depth + lanes), BF16),
            pltpu.VMEM((n_dp, cap, depth + lanes), BF16),
            pltpu.VMEM((n_dp * cap, spread_w), F32),
            pltpu.VMEM((n_dp * cap // 2, lanes), BF16),
            pltpu.VMEM((n_t, n_dp * cap // 2, lanes), BF16),
            pltpu.VMEM((n_dp, nch, cap, chunk), BF16),
            pltpu.VMEM((n_dp, nch, cap, chunk), BF16),
            pltpu.VMEM((n_t, nch, rows, chunk), BF16),
            pltpu.VMEM((n_t + 1, nch, rows, chunk), BF16),
            pltpu.VMEM((nch, rows, chunk), F32),
            dma((n_t, nch)),
            dma((3,)),
            dma((n_dp,)),
            dma((n_dp,)),
            dma((n_t,)),
            dma((n_t,)),
            dma((n_dp, nch)),
            dma((n_dp, nch)),
            dma((n_t, nch)),
            dma((n_t + 1, nch)),
        ],
        compiler_params=pltpu.CompilerParams(
            collective_id=0, has_side_effects=True, vmem_limit_bytes=56 * 1024 * 1024
        ),
    )(attended, request_adapter_index[None, :], adapter_row_table[None, :], output_weight, down, up)


def solution(mesh):
    in_specs = (
        P(("groups", "dp"), "tensor"),
        P("tensor", None),
        P("dp", "tensor", None),
        P("dp", None, "tensor"),
        P(("groups", "dp")),
        P("groups"),
    )
    out_specs = P(("groups", "dp"), "tensor")
    body = functools.partial(local, mesh.shape["dp"], mesh.shape["tensor"])
    return jax.shard_map(body, mesh=mesh, in_specs=in_specs, out_specs=out_specs, check_vma=False)
```
